256 devices in a mesh: island: 16 (over z_hi, y), fsdp: 16 (over x, z_lo, core).
Axes of the slice: x: 4, y: 4, z: 8 (z_hi: 4, z_lo: 2; z = z_hi * 2 + z_lo), core: 2. Of those that a mesh axis runs over, the one named last changes fastest.
Arguments:
- tokens: bfloat16 [131072, 8192], P(('island', 'fsdp')), may hold values from -6 to 6
- input_norm_gain: bfloat16 [8192], replicated, may hold values from 0.099609375 to 1.8984375
- key_value_weight: bfloat16 [8192, 1024], P('fsdp'), may hold values from -0.0625 to 0.0625
- adapter_down_factors: bfloat16 [16, 8192, 128], P('island', 'fsdp'), may hold values from -0.0625 to 0.0625
- adapter_up_factors: bfloat16 [16, 2, 64, 512], P('island'), may hold values from -0.75 to 0.75
Outputs:
- keys_values: bfloat16 [131072, 1024], P(('island', 'fsdp'))
The draws below stay inside these ranges and needn't reach their ends.
All inputs are finite; a program needn't handle non-finite values.
Results may differ from the reference program's by a relative error of at most 0.0058.
Values may be sent and summed in bfloat16 or wider, within the bound.
No kernel may reach another device: no remote copies, remote signals or barrier semaphores. Data moves between devices by JAX's collectives and lax.ppermute only.
A program may use at most 128 MiB of HBM per device.

```python
import jax
import jax.numpy as jnp
from jax import lax

MODEL_WIDTH = 8192
ADAPTER_RANK = 64
TOK_DEV = 512
HALF_COLUMNS = 512
KVW = 1024
ISLAND_COUNT = 16
TOKENS = 131072


def levels(stream_key, extent, pieces, low, top_value):
    loudness, own = 1.0, jax.random.fold_in(stream_key, 6)
    for axis_at, parts in pieces:
        draws = jnp.exp(jax.random.uniform(jax.random.fold_in(own, axis_at), (parts,), jnp.float32, low / len(pieces), top_value / len(pieces)))
        loudness = loudness * jnp.repeat(draws, extent[axis_at] // parts).reshape([-1 if axis == axis_at else 1 for axis in range(len(extent))])
    return loudness


def centred(own_key, shape, width, most, split=(), kind=jnp.bfloat16):
    level = levels(own_key, shape, split, -0.22, 0.18) if split else 1.0
    array = jax.random.normal(own_key, shape, jnp.float32) * width * level
    return jnp.minimum(jnp.maximum(array, -most), most).astype(kind)


def setup_inputs(seed: int = 0) -> dict:
    arg_keys = jax.random.split(jax.random.key(seed), 6)
    return {
        "tokens": centred(arg_keys[0], (TOKENS, MODEL_WIDTH), 1.0, 6.0, ((0, 256),)),
        "input_norm_gain": jnp.clip(1.0 + 0.18 * jax.random.normal(arg_keys[1], (MODEL_WIDTH,), jnp.float32), 0.099609375, 1.8984375).astype(jnp.bfloat16),
        "key_value_weight": centred(arg_keys[2], (MODEL_WIDTH, KVW), MODEL_WIDTH ** -0.5, 0.0625, ((0, 16),)),
        "adapter_down_factors": centred(arg_keys[3], (ISLAND_COUNT, MODEL_WIDTH, 2 * ADAPTER_RANK), MODEL_WIDTH ** -0.5, 0.0625, ((0, 16), (1, 16))),
        "adapter_up_factors": centred(arg_keys[4], (ISLAND_COUNT, 2, ADAPTER_RANK, HALF_COLUMNS), ADAPTER_RANK ** -0.5, 0.75, ((0, 16),)),
    }


def reference(tokens, input_norm_gain, key_value_weight, adapter_down_factors, adapter_up_factors):
    down_factors_all = adapter_down_factors.astype(jnp.float32).reshape(ISLAND_COUNT, MODEL_WIDTH, 2, ADAPTER_RANK)
    up_factors_all = adapter_up_factors.astype(jnp.float32)
    update = jnp.einsum('idhr,ihrk->dhk', down_factors_all, up_factors_all).reshape(MODEL_WIDTH, KVW)
    merged = (key_value_weight.astype(jnp.float32) + 0.25 * update).astype(jnp.bfloat16)
    gain_f = input_norm_gain.astype(jnp.float32)

    def project(block):
        values = block.astype(jnp.float32)
        meansq = lax.optimization_barrier(jnp.mean(values * values, axis=-1, keepdims=True))
        normed = (values * lax.rsqrt(meansq + 1e-05) * gain_f).astype(jnp.bfloat16)
        return jnp.dot(normed, merged, preferred_element_type=jnp.float32).astype(jnp.bfloat16)
    blocks = tokens.reshape(TOKENS // TOK_DEV, TOK_DEV, MODEL_WIDTH)
    return lax.map(project, blocks).reshape(TOKENS, KVW)
```

```python
import jax
import jax.numpy as jnp
from jax import lax
from jax.experimental import pallas as pl
from jax.experimental.pallas import tpu as pltpu
from jax.sharding import Mesh, PartitionSpec as P

AXES = ("zh", "y", "x", "zl", "c")
SIZES = (4, 4, 4, 2, 2)
RANK = 64
HALF = 512
EPS = 1e-05
F32 = jnp.float32
BF16 = jnp.bfloat16


def pairs(move):
    out = []
    for src in range(256):
        core, rest = src % 2, src // 2
        zl, rest = rest % 2, rest // 2
        x, rest = rest % 4, rest // 4
        y, zh = rest % 4, rest // 4
        zh2, y2, x2, zl2, core2 = move(zh, y, x, zl, core)
        out.append((src, (((zh2 % 4 * 4 + y2 % 4) * 4 + x2 % 4) * 2 + zl2) * 2 + core2))
    return out


def send(array, move):
    return lax.ppermute(array, AXES, pairs(move))


def to_core(zh, y, x, zl, c):
    return zh, y, x, zl, 1 - c


def to_zl(zh, y, x, zl, c):
    return zh, y, x, 1 - zl, c


def along_y(k):
    return lambda zh, y, x, zl, c: (zh, y + k, x, zl, c)


def along_zh(k):
    return lambda zh, y, x, zl, c: (zh + k, y, x, zl, c)


def first(k):
    return lambda zh, y, x, zl, c: (zh, y + k, x, zl, c) if c == 0 else (zh, y, x + k, zl, c)


def last(k):
    return lambda zh, y, x, zl, c: (zh, y, x + k, zl, c) if c == 0 else (zh, y + k, x, zl, c)


VMEM = pl.BlockSpec(memory_space=pltpu.VMEM)
SMEM = pl.BlockSpec(memory_space=pltpu.SMEM)


def shape(rows, columns, dtype=BF16):
    return jax.ShapeDtypeStruct((rows, columns), dtype)


def call(body, place, operands, outs, scratch=(), cost=1 << 20):
    return pl.pallas_call(
        body,
        out_shape=outs,
        in_specs=[SMEM] + [VMEM] * len(operands),
        out_specs=jax.tree.map(lambda _: VMEM, outs),
        scratch_shapes=list(scratch),
        cost_estimate=pl.CostEstimate(flops=cost, bytes_accessed=cost, transcendentals=0),
    )(place, *operands)


def prepare(place, own, other, up, *rest):
    outs, packed = rest[:4], rest[4]
    y, c = place[1], place[4]
    swapped = pltpu.roll(other[...].astype(F32), RANK, 1)
    lane = lax.broadcasted_iota(jnp.int32, swapped.shape, 1)
    mine = (lane < RANK) == (c == 0)
    packed[...] = jnp.where(mine, own[...].astype(F32), swapped).astype(BF16)
    factor = up[pl.ds(c, 1)][0]
    for k in range(4):
        block = lax.rem(y + k, 4)
        outs[k][0:64, :] = factor
        for j in range(4):
            start = pl.multiple_of(block * 128 + j * 32, 32)
            outs[k][64:96, j * 128 : (j + 1) * 128] = packed[pl.ds(start, 32), :]


def partial_sums(place, *rest):
    parts, outs, total = rest[:4], rest[4:8], rest[8]
    zh = place[0]
    lane = lax.broadcasted_iota(jnp.int32, (128, 128), 1)
    zero = jnp.zeros((128, 128), BF16)
    lefts, rights = [], []
    for part in parts:
        down = jnp.concatenate([part[64:96, j * 128 : (j + 1) * 128] for j in range(4)], axis=0)
        low = jnp.where(lane < RANK, down, zero)
        high = jnp.where(lane < RANK, zero, down)
        lefts.append(jnp.concatenate([low, high], axis=0))
        factor = part[0:64, :]
        rights.append(jnp.concatenate([factor, factor], axis=0))
    value = None
    for k in (0, 2):
        left = jnp.concatenate(lefts[k : k + 2], axis=1)
        right = jnp.concatenate(rights[k : k + 2], axis=0)
        term = jnp.dot(left, right, preferred_element_type=F32)
        value = term if value is None else value + term
    total[...] = value
    for k in range(4):
        start = pl.multiple_of(lax.rem(zh + k, 4) * 32, 32)
        outs[k][0:32, :] = total[pl.ds(start, 32), :]
        outs[k][32:64, :] = total[pl.ds(start + 128, 32), :]


def merge(place, own, other, a, b, c, d, out):
    core = place[4]
    mine, theirs = own[...].astype(F32), other[...].astype(F32)
    update = 0.25 * ((a[...] + b[...]) + (c[...] + d[...]))
    out[0:32, :] = (jnp.where(core == 0, mine, theirs) + update[0:32]).astype(BF16)
    out[32:64, :] = (jnp.where(core == 0, theirs, mine) + update[32:64]).astype(BF16)


def assemble(place, *rest):
    parts, out = rest[:4], rest[4]
    zh = place[0]
    for k in range(4):
        start = pl.multiple_of(lax.rem(zh + 4 - k, 4) * 32, 32)
        out[pl.ds(start, 32), :] = parts[k][0:32, :]
        out[pl.ds(start + 128, 32), :] = parts[k][32:64, :]


def join(place, *rest):
    parts, out = rest[:4], rest[4]
    for k in range(4):
        out[k * 256 : (k + 1) * 256, :] = parts[k][...]


def norm_body(table, tokens, gain, *outs):
    rows = tokens.shape[0]
    squares = jnp.zeros((rows, 128), F32)
    for g in range(64):
        value = tokens[:, g * 128 : (g + 1) * 128].astype(F32)
        squares = squares + value * value
    mean = jnp.sum(squares, axis=1, keepdims=True) / 8192.0
    scale = jnp.broadcast_to(lax.rsqrt(mean + EPS), (rows, 128))
    for g in range(64):
        at = pl.ds(pl.multiple_of(table[g] * 128, 128), 128)
        value = tokens[:, at].astype(F32) * scale * gain[:, at].astype(F32)
        outs[g // 8][:, (g % 8) * 128 : (g % 8 + 1) * 128] = value.astype(BF16)


def normalise(table, tokens, gain):
    rows = 64
    return pl.pallas_call(
        norm_body,
        grid=(512 // rows,),
        out_shape=[shape(512, 1024)] * 8,
        in_specs=[
            SMEM,
            pl.BlockSpec((rows, 8192), lambda i: (i, 0)),
            pl.BlockSpec((1, 8192), lambda i: (0, 0)),
        ],
        out_specs=[pl.BlockSpec((rows, 1024), lambda i: (i, 0))] * 8,
        cost_estimate=pl.CostEstimate(flops=1 << 24, bytes_accessed=1 << 24, transcendentals=0),
    )(table, tokens, gain.reshape(1, 8192))


def feature_order(y, x, zl, c):
    place = jnp.arange(64, dtype=jnp.int32)
    block, part, step, core = place // 16, place // 8 % 2, place // 2 % 4, place % 2
    far = jnp.where(c == 0, x, y)
    near = jnp.where(c == 0, y, x)
    far = (far + 4 - block) % 4
    near = (near + 4 - step) % 4
    row_x = jnp.where(c == 0, far, near)
    row_y = jnp.where(c == 0, near, far)
    return row_x * 16 + (zl ^ part) * 8 + core * 4 + row_y


def per_device(tokens, gain, weight, down, up):
    zh, y, x, zl, c = (lax.axis_index(a) for a in AXES)
    place = jnp.stack([zh, y, x, zl, c]).astype(jnp.int32)
    down, up = down[0], up[0]

    down_other = send(down, to_core)
    row = y * 128 + zh * 32
    weight_own = lax.dynamic_slice(weight, (row, c * HALF), (32, HALF))
    weight_other = send(lax.dynamic_slice(weight, (row, (1 - c) * HALF), (32, HALF)), to_core)

    parts = call(prepare, place, (down, down_other, up), [shape(96, HALF)] * 4, [pltpu.VMEM((512, 128), BF16)])
    parts = [parts[0]] + [send(parts[k], along_y(k)) for k in (1, 3, 2)]
    sums = call(partial_sums, place, parts, [shape(64, HALF, F32)] * 4, [pltpu.VMEM((256, HALF), F32)])
    sums = [sums[0]] + [send(sums[k], along_zh(k)) for k in (1, 3, 2)]
    merged = call(merge, place, (weight_own, weight_other, *sums), shape(64, HALF))
    near = [merged] + [send(merged, along_zh(k)) for k in (1, 2, 3)]
    chunk = call(assemble, place, near, shape(256, HALF))

    tokens_other = send(tokens, to_core)
    table = feature_order(y, x, zl, c)
    normed = normalise(table, tokens, gain)
    normed_other = normalise(table, tokens_other, gain)

    blocks = {}
    for part, piece in ((0, chunk), (1, send(chunk, to_zl))):
        pieces = [piece] + [send(piece, first(k)) for k in (1, 2, 3)]
        blocks[0, part] = call(join, place, pieces, shape(1024, HALF))
    for part in (0, 1):
        blocks[1, part] = send(blocks[0, part], last(1))
        blocks[3, part] = send(blocks[0, part], last(-1))
    blocks[2, 0] = send(blocks[1, 0], last(1))
    blocks[2, 1] = send(blocks[3, 1], last(-1))

    mine = theirs = None
    for block in (0, 1, 3, 2):
        for part in (0, 1):
            rows = blocks[block, part]
            term = jnp.dot(normed_other[block * 2 + part], rows, preferred_element_type=F32)
            theirs = term if theirs is None else theirs + term
            term = jnp.dot(normed[block * 2 + part], rows, preferred_element_type=F32)
            mine = term if mine is None else mine + term
    back = send(theirs.astype(BF16), to_core)
    mine = mine.astype(BF16)
    left = jnp.where(c == 0, mine, back)
    right = jnp.where(c == 0, back, mine)
    return jnp.concatenate([left, right], axis=1)


def solution(mesh):
    fine = Mesh(mesh.devices.reshape(SIZES), AXES)
    rows = ("x", "zl", "c")
    placed = (
        P(AXES, None),
        P(),
        P(rows, None),
        P(("zh", "y"), rows, None),
        P(("zh", "y"), None, None, None),
    )
    return jax.shard_map(per_device, mesh=fine, in_specs=placed, out_specs=P(AXES, None), check_vma=False)
```

```python
import functools

import jax
import jax.numpy as jnp
from jax import lax
from jax.experimental import pallas as pl
from jax.experimental.pallas import tpu as pltpu
from jax.sharding import Mesh, PartitionSpec as P

AXES = ("zh", "y", "x", "zl", "c")
SIZES = (4, 4, 4, 2, 2)
RANK = 64
HALF = 512
EPS = 1e-05
FEATURES = 8192
F32 = jnp.float32
BF16 = jnp.bfloat16


def pairs(move):
    out = []
    for src in range(256):
        core, rest = src % 2, src // 2
        zl, rest = rest % 2, rest // 2
        x, rest = rest % 4, rest // 4
        y, zh = rest % 4, rest // 4
        zh2, y2, x2, zl2, core2 = move(zh, y, x, zl, core)
        out.append((src, (((zh2 % 4 * 4 + y2 % 4) * 4 + x2 % 4) * 2 + zl2) * 2 + core2))
    return out


def send(array, move):
    return lax.ppermute(array, AXES, pairs(move))


def to_core(zh, y, x, zl, c):
    return zh, y, x, zl, 1 - c


def beside(zh, y, x, zl, c):
    if c == 0:
        return zh, y, x, 1 - zl, c
    return (zh - 1, y, x, 1, c) if zl == 0 else (zh + 1, y, x, 0, c)


def along_zh(k):
    return lambda zh, y, x, zl, c: (zh + k, y, x, zl, c)


def along_y(k):
    return lambda zh, y, x, zl, c: (zh, y + k, x, zl, c)


def first(k):
    return lambda zh, y, x, zl, c: (zh, y + k, x, zl, c) if c == 0 else (zh, y, x + k, zl, c)


def last(k):
    return lambda zh, y, x, zl, c: (zh, y, x + k, zl, c) if c == 0 else (zh, y + k, x, zl, c)


def after(array, *others):
    return lax.optimization_barrier((array, *others))[0]


VMEM = pl.BlockSpec(memory_space=pltpu.VMEM)


def call(body, operands, outs, scratch=(), cost=1024, flops=1024, free=()):
    operands = [
        pltpu.with_memory_space_constraint(a, pltpu.HBM if i in free else pltpu.VMEM) for i, a in enumerate(operands)
    ]
    return pl.pallas_call(
        body,
        out_shape=outs,
        in_specs=[VMEM] * len(operands),
        out_specs=jax.tree.map(lambda _: VMEM, outs),
        scratch_shapes=list(scratch),
        compiler_params=pltpu.CompilerParams(vmem_limit_bytes=16 << 20),
        cost_estimate=pl.CostEstimate(flops=flops, bytes_accessed=cost, transcendentals=0),
    )(*operands)


def prepare(own, other, up, *rest):
    outs, packed = rest[:4], rest[4]
    zh, c = lax.axis_index("zh"), lax.axis_index("c")
    mine, theirs = own[...].astype(F32), other[...].astype(F32)
    turned = jnp.where(c == 0, theirs, mine)
    turned = pltpu.roll(turned, RANK, 1)
    lane = lax.broadcasted_iota(jnp.int32, mine.shape, 1)
    low = jnp.where(c == 0, mine, turned)
    high = jnp.where(c == 0, turned, theirs)
    packed[...] = jnp.where(lane < RANK, low, high).astype(BF16)
    factor = up[pl.ds(c, 1)][0]
    for k in range(4):
        start = lax.rem(zh + k, 4) * 32
        outs[k][0:64, :] = factor
        for y in range(4):
            rows = pl.ds(pl.multiple_of(start + y * 128, 32), 32)
            outs[k][64:96, y * 128 : (y + 1) * 128] = packed[rows, :]


def partial_sums(*rest):
    parts, outs, total = rest[:4], rest[4:8], rest[8]
    y = lax.axis_index("y")
    lane = lax.broadcasted_iota(jnp.int32, (128, 128), 1)
    zero = jnp.zeros((128, 128), BF16)
    lefts, rights = [], []
    for part in parts:
        down = jnp.concatenate([part[64:96, j * 128 : (j + 1) * 128] for j in range(4)], axis=0)
        low = jnp.where(lane < RANK, down, zero)
        high = jnp.where(lane < RANK, zero, down)
        lefts.append(jnp.concatenate([low, high], axis=0))
        rights += [part[0:64, :]] * 2
    left = jnp.concatenate(lefts, axis=1)
    right = jnp.concatenate(rights, axis=0)
    total[...] = jnp.dot(left, right, preferred_element_type=F32)
    for k in range(4):
        start = pl.multiple_of(lax.rem(y + k, 4) * 32, 32)
        outs[k][0:32, :] = total[pl.ds(start, 32), :]
        outs[k][32:64, :] = total[pl.ds(start + 128, 32), :]


def merge(own, other, gain, a, b, c, d, out):
    update = 0.25 * ((a[...] + b[...]) + (c[...] + d[...]))
    out[0:32, :] = ((own[...].astype(F32) + update[0:32]) * gain[0:32]).astype(BF16)
    out[32:64, :] = ((other[...].astype(F32) + update[32:64]) * gain[32:64]).astype(BF16)


def assemble(*refs):
    parts, out = refs[:4], refs[4]
    zh = lax.axis_index("zh")
    for k in range(4):
        start = pl.multiple_of(lax.rem(zh + 4 - k, 4) * 32, 32)
        out[pl.ds(start, 32), :] = parts[k][0:32, :]
        out[pl.ds(start + 128, 32), :] = parts[k][32:64, :]


def join(*refs):
    parts, whole, mine, theirs = refs[:4], refs[4], refs[5], refs[6]
    for k in range(4):
        at, below = slice(k * 128, (k + 1) * 128), slice(512 + k * 128, 512 + (k + 1) * 128)
        whole[at, :] = mine[at, :] = parts[k][0:128, :]
        whole[below, :] = theirs[at, :] = parts[k][128:256, :]


def upper(rows, out):
    out[...] = rows[0:512, :]


def strip(place):
    y, x, zl, c = (lax.axis_index(a) for a in AXES[1:])
    block, part, core, step = place // 16, place // 8 % 2, place // 4 % 2, place % 4
    far = jnp.where(c == 0, x, y)
    near = jnp.where(c == 0, y, x)
    far = lax.rem(far + 4 - block, 4)
    near = lax.rem(near + 4 - step, 4)
    row_x = jnp.where(c == 0, far, near)
    row_y = jnp.where(c == 0, near, far)
    zl = zl if part == 0 else 1 - zl
    core = c if core == 0 else 1 - c
    return row_x * 16 + zl * 8 + core * 4 + row_y


TALL = 64
SHARE = 256


def stage_body(tokens, out, scale):
    at = pl.ds(pl.multiple_of(pl.program_id(0) * TALL, TALL), TALL)
    square = jnp.zeros((TALL, 128), F32)
    for place in range(64):
        column = pl.ds(pl.multiple_of(strip(place) * 128, 128), 128)
        piece = tokens[:, column]
        out[at, place * 128 : (place + 1) * 128] = piece
        value = piece.astype(F32)
        square = square + value * value
    mean = jnp.sum(square, axis=1, keepdims=True) / FEATURES
    scale[at, :] = jnp.broadcast_to(lax.rsqrt(mean + EPS), (TALL, 128))


def stage(tokens, share):
    steps = SHARE // TALL
    return pl.pallas_call(
        stage_body,
        grid=(steps,),
        out_shape=[pltpu.VMEM((SHARE, FEATURES), BF16), pltpu.VMEM((SHARE, 128), F32)],
        in_specs=[pl.BlockSpec((TALL, FEATURES), lambda i: (i + share * steps, 0))],
        out_specs=[VMEM] * 2,
        compiler_params=pltpu.CompilerParams(vmem_limit_bytes=16 << 20),
        cost_estimate=pl.CostEstimate(flops=1024, bytes_accessed=1024, transcendentals=0),
    )(pltpu.with_memory_space_constraint(tokens, pltpu.HBM))


def product_body(opening, closing, ats, *refs):
    shares = 2 if closing else 4
    tokens, rows, refs = refs[:shares], refs[shares : shares + len(ats)], refs[shares + len(ats) :]
    if not opening:
        sums, refs = refs[0], refs[1:]
    if closing:
        scales, refs = refs[:2], refs[2:]
    for who in range(shares):
        tall = slice(who * SHARE, (who + 1) * SHARE)
        past = slice((who + closing * 2 - 2) * SHARE, (who + closing * 2 - 1) * SHARE) if closing else tall
        total = None if opening else sums[past, :]
        for at, some in zip(ats, rows):
            term = jnp.dot(tokens[who][:, at : at + some.shape[0]], some[...], preferred_element_type=F32)
            total = term if total is None else total + term
        if closing:
            refs[0][tall, :] = (total * scales[who][:, 0:1]).astype(BF16)
        else:
            refs[0][tall, :] = total


def product(tokens, rows, state, ats, scales=(), closing=0):
    opening = state is None
    out = pltpu.VMEM((512, HALF), BF16) if closing else pltpu.VMEM((1024, HALF), F32)
    body = functools.partial(product_body, opening, closing, ats)
    operands = (*tokens, *rows, *(() if opening else (state,)), *scales)
    return call(body, operands, out)


def combine(own, other, out):
    c = lax.axis_index("c")

    @pl.when(c == 0)
    def _():
        out[:, 0:HALF] = own[...]
        out[:, HALF:] = other[...]

    @pl.when(c == 1)
    def _():
        out[:, 0:HALF] = other[...]
        out[:, HALF:] = own[...]


def per_device(tokens, gain, weight, down, up):
    zh, y, x, zl, c = (lax.axis_index(a) for a in AXES)
    down, up = down[0], up[0]

    down_other = send(down, to_core)
    parts = call(
        prepare,
        (down, down_other, up),
        [pltpu.VMEM((96, HALF), BF16)] * 4,
        [pltpu.VMEM((512, 128), BF16)],
        free=(0, 2),
    )
    parts = [parts[0]] + [send(parts[k], along_zh(k)) for k in (2, 1, 3)]

    row = y * 128 + zh * 32
    weight_own = lax.dynamic_slice(weight, (row, c * HALF), (32, HALF))
    weight_other = lax.dynamic_slice(weight, (row, (1 - c) * HALF), (32, HALF))
    weight_other = send(after(weight_other, parts[1]), to_core)
    tokens_other = send(after(tokens, down_other), to_core)
    start = (x * 2 + zl) * 1024 + row
    gains = [lax.dynamic_slice(gain, (start + who * HALF,), (32,)) for who in (c, 1 - c)]
    gains = jnp.broadcast_to(jnp.concatenate(gains).astype(F32)[:, None], (64, HALF))

    staged = [stage(after(tokens, parts[0]), 0), stage(tokens, 1), stage(tokens_other, 0), stage(tokens_other, 1)]
    every, scales = zip(*staged)

    parts = [after(parts[0], every[0]), *parts[1:]]
    sums = call(partial_sums, parts, [pltpu.VMEM((64, HALF), F32)] * 4, [pltpu.VMEM((256, HALF), F32)])
    sums = [sums[0]] + [send(sums[k], along_y(k)) for k in (1, 3, 2)]
    sums = [after(sums[0], every[1]), *sums[1:]]
    merged = call(merge, (weight_own, weight_other, gains, *sums), pltpu.VMEM((64, HALF), BF16))
    merged = [merged] + [send(merged, along_zh(k)) for k in (2, 1, 3)]
    merged = [after(merged[0], every[2]), merged[2], merged[1], merged[3]]
    chunk = call(assemble, merged, pltpu.VMEM((256, HALF), BF16))

    whole, slab = pltpu.VMEM((1024, HALF), BF16), pltpu.VMEM((512, HALF), BF16)
    near = [send(chunk, first(k)) for k in (1, 2, 3)]
    here0, up0, low0 = call(join, [after(chunk, every[3]), *near], [whole, slab, slab])

    here1 = send(here0, beside)
    left_low0, right_low0 = send(low0, last(-1)), send(low0, last(1))
    left_up0, right_up0 = send(up0, last(-1)), send(up0, last(1))
    state = product(every, (here0,), None, (0,))
    left_low0 = after(left_low0, state)
    left_low1 = send(left_low0, beside)
    right_low0 = after(right_low0, left_low0)
    right_low1 = send(right_low0, beside)
    here1 = after(here1, right_low0)
    up1 = call(upper, (here1,), slab)
    right_up1 = send(up1, last(1))
    left_up0 = after(left_up0, up1)
    left_up1 = send(after(up1, left_up0), last(-1))
    state = product(every, (here1,), after(state, left_up0), (1024,))
    right_up0 = after(right_up0, state)
    far_up0 = send(right_up0, last(1))
    left_low1 = after(left_low1, right_up0)
    far_low0 = send(after(left_low0, left_low1), last(-1))
    state = product(every, (left_up0, left_low0), after(state, left_low1), (6144, 6656))
    state = product(every, (right_up0, right_low0), state, (2048, 2560))
    right_up1 = after(right_up1, state)
    far_up1 = send(right_up1, last(1))
    left_up1 = after(left_up1, right_up1)
    far_low1 = send(after(left_low1, left_up1), last(-1))
    right_low1 = after(right_low1, left_up1)
    state = product(every, (right_up1, right_low1), after(state, right_low1), (3072, 3584))
    state = product(every, (left_up1, left_low1), state, (7168, 7680))
    far_up0 = after(far_up0, state)
    far_low0 = after(far_low0, far_up0)
    state = product(every, (far_up0, far_low0), state, (4096, 4608))
    far_up1 = after(far_up1, state)
    ending, ats = (far_up1, far_low1), (5120, 5632)
    theirs = product(every[2:], ending, state, ats, scales[2:], 2)
    back = send(theirs, to_core)
    mine = product(every[:2], ending, state, ats, scales[:2], 1)
    return call(combine, (mine, back), shape(512, 2 * HALF))


def shape(rows, columns, dtype=BF16):
    return jax.ShapeDtypeStruct((rows, columns), dtype)


def solution(mesh):
    fine = Mesh(mesh.devices.reshape(SIZES), AXES)
    rows = ("x", "zl", "c")
    placed = (
        P(AXES, None),
        P(),
        P(rows, None),
        P(("zh", "y"), rows, None),
        P(("zh", "y"), None, None, None),
    )
    return jax.shard_map(per_device, mesh=fine, in_specs=placed, out_specs=P(AXES, None), check_vma=False)
```

```python
import functools

import jax
import jax.numpy as jnp
from jax import lax
from jax.experimental import pallas as pl
from jax.experimental.pallas import tpu as pltpu
from jax.sharding import Mesh, PartitionSpec as P

AXES = ("zh", "y", "x", "zl", "c")
SIZES = (4, 4, 4, 2, 2)
RANK = 64
HALF = 512
EPS = 1e-05
FEATURES = 8192
F32 = jnp.float32
BF16 = jnp.bfloat16


def pairs(move):
    out = []
    for src in range(256):
        core, rest = src % 2, src // 2
        zl, rest = rest % 2, rest // 2
        x, rest = rest % 4, rest // 4
        y, zh = rest % 4, rest // 4
        zh2, y2, x2, zl2, core2 = move(zh, y, x, zl, core)
        out.append((src, (((zh2 % 4 * 4 + y2 % 4) * 4 + x2 % 4) * 2 + zl2) * 2 + core2))
    return out


def send(array, move):
    return lax.ppermute(array, AXES, pairs(move))


def to_core(zh, y, x, zl, c):
    return zh, y, x, zl, 1 - c


def beside(zh, y, x, zl, c):
    if c == 0:
        return zh, y, x, 1 - zl, c
    return (zh - 1, y, x, 1, c) if zl == 0 else (zh + 1, y, x, 0, c)


def along_zh(k):
    return lambda zh, y, x, zl, c: (zh + k, y, x, zl, c)


def along_y(k):
    return lambda zh, y, x, zl, c: (zh, y + k, x, zl, c)


def first(k):
    return lambda zh, y, x, zl, c: (zh, y + k, x, zl, c) if c == 0 else (zh, y, x + k, zl, c)


def last(k):
    return lambda zh, y, x, zl, c: (zh, y, x + k, zl, c) if c == 0 else (zh, y + k, x, zl, c)


def after(array, *others):
    return lax.optimization_barrier((array, *others))[0]


VMEM = pl.BlockSpec(memory_space=pltpu.VMEM)
HBM = pl.BlockSpec(memory_space=pltpu.HBM)


def call(body, operands, outs, scratch=(), cost=1024, flops=1024, free=(), far=()):
    operands = [
        pltpu.with_memory_space_constraint(a, pltpu.HBM if i in free + far else pltpu.VMEM)
        for i, a in enumerate(operands)
    ]
    return pl.pallas_call(
        body,
        out_shape=outs,
        in_specs=[HBM if i in far else VMEM for i in range(len(operands))],
        out_specs=jax.tree.map(lambda _: VMEM, outs),
        scratch_shapes=list(scratch),
        compiler_params=pltpu.CompilerParams(vmem_limit_bytes=16 << 20),
        cost_estimate=pl.CostEstimate(flops=flops, bytes_accessed=cost, transcendentals=0),
    )(*operands)


def prepare(own, other, up, weight, *rest):
    outs, kept, given, packed, arrived = rest[:4], rest[4], rest[5], rest[6], rest[7]
    y, zh, c = lax.axis_index("y"), lax.axis_index("zh"), lax.axis_index("c")
    rows = pl.ds(pl.multiple_of(y * 128 + zh * 32, 32), 32)
    copies = []
    for out, half in ((kept, c), (given, 1 - c)):
        columns = pl.ds(pl.multiple_of(half * HALF, HALF), HALF)
        copies.append(pltpu.make_async_copy(weight.at[rows, columns], out, arrived.at[len(copies)]))
        copies[-1].start()
    mine, theirs = own[...].astype(F32), other[...].astype(F32)
    turned = jnp.where(c == 0, theirs, mine)
    turned = pltpu.roll(turned, RANK, 1)
    lane = lax.broadcasted_iota(jnp.int32, mine.shape, 1)
    low = jnp.where(c == 0, mine, turned)
    high = jnp.where(c == 0, turned, theirs)
    packed[...] = jnp.where(lane < RANK, low, high).astype(BF16)
    factor = up[pl.ds(c, 1)][0]
    for k in range(4):
        start = lax.rem(zh + k, 4) * 32
        outs[k][0:64, :] = factor
        for y in range(4):
            rows = pl.ds(pl.multiple_of(start + y * 128, 32), 32)
            outs[k][64:96, y * 128 : (y + 1) * 128] = packed[rows, :]
    for copy in copies:
        copy.wait()


def partial_sums(*rest):
    parts, outs, total = rest[:4], rest[4:8], rest[8]
    y = lax.axis_index("y")
    lane = lax.broadcasted_iota(jnp.int32, (128, 128), 1)
    zero = jnp.zeros((128, 128), BF16)
    lefts, rights = [], []
    for part in parts:
        down = jnp.concatenate([part[64:96, j * 128 : (j + 1) * 128] for j in range(4)], axis=0)
        low = jnp.where(lane < RANK, down, zero)
        high = jnp.where(lane < RANK, zero, down)
        lefts.append(jnp.concatenate([low, high], axis=0))
        rights += [part[0:64, :]] * 2
    left = jnp.concatenate(lefts, axis=1)
    right = jnp.concatenate(rights, axis=0)
    total[...] = jnp.dot(left, right, preferred_element_type=F32)
    for k in range(4):
        start = pl.multiple_of(lax.rem(y + k, 4) * 32, 32)
        outs[k][0:32, :] = total[pl.ds(start, 32), :]
        outs[k][32:64, :] = total[pl.ds(start + 128, 32), :]


def merge(own, other, gain, a, b, c, d, out):
    update = 0.25 * ((a[...] + b[...]) + (c[...] + d[...]))
    out[0:32, :] = ((own[...].astype(F32) + update[0:32]) * gain[0:32]).astype(BF16)
    out[32:64, :] = ((other[...].astype(F32) + update[32:64]) * gain[32:64]).astype(BF16)


def assemble(*refs):
    parts, out = refs[:4], refs[4]
    zh = lax.axis_index("zh")
    for k in range(4):
        start = pl.multiple_of(lax.rem(zh + 4 - k, 4) * 32, 32)
        out[pl.ds(start, 32), :] = parts[k][0:32, :]
        out[pl.ds(start + 128, 32), :] = parts[k][32:64, :]


def join(*refs):
    parts, whole, mine, theirs = refs[:4], refs[4], refs[5], refs[6]
    for k in range(4):
        at, below = slice(k * 128, (k + 1) * 128), slice(512 + k * 128, 512 + (k + 1) * 128)
        whole[at, :] = mine[at, :] = parts[k][0:128, :]
        whole[below, :] = theirs[at, :] = parts[k][128:256, :]


def upper(rows, out):
    out[...] = rows[0:512, :]


def strip(place):
    y, x, zl, c = (lax.axis_index(a) for a in AXES[1:])
    block, part, core, step = place // 16, place // 8 % 2, place // 4 % 2, place % 4
    far = jnp.where(c == 0, x, y)
    near = jnp.where(c == 0, y, x)
    far = lax.rem(far + 4 - block, 4)
    near = lax.rem(near + 4 - step, 4)
    row_x = jnp.where(c == 0, far, near)
    row_y = jnp.where(c == 0, near, far)
    zl = zl if part == 0 else 1 - zl
    core = c if core == 0 else 1 - c
    return row_x * 16 + zl * 8 + core * 4 + row_y


TALL = 64
SHARE = 256


def stage_body(tokens, out, scale):
    at = pl.ds(pl.multiple_of(pl.program_id(0) * TALL, TALL), TALL)
    square = jnp.zeros((TALL, 128), F32)
    for place in range(64):
        column = pl.ds(pl.multiple_of(strip(place) * 128, 128), 128)
        piece = tokens[:, column]
        out[at, place * 128 : (place + 1) * 128] = piece
        value = piece.astype(F32)
        square = square + value * value
    mean = jnp.sum(square, axis=1, keepdims=True) / FEATURES
    scale[at, :] = jnp.broadcast_to(lax.rsqrt(mean + EPS), (TALL, 128))


def stage(tokens, share):
    steps = SHARE // TALL
    return pl.pallas_call(
        stage_body,
        grid=(steps,),
        out_shape=[pltpu.VMEM((SHARE, FEATURES), BF16), pltpu.VMEM((SHARE, 128), F32)],
        in_specs=[pl.BlockSpec((TALL, FEATURES), lambda i: (i + share * steps, 0))],
        out_specs=[VMEM] * 2,
        compiler_params=pltpu.CompilerParams(vmem_limit_bytes=16 << 20),
        cost_estimate=pl.CostEstimate(flops=1024, bytes_accessed=1024, transcendentals=0),
    )(pltpu.with_memory_space_constraint(tokens, pltpu.HBM))


def product_body(opening, closing, ats, *refs):
    shares = 2 if closing else 4
    tokens, rows, refs = refs[:shares], refs[shares : shares + len(ats)], refs[shares + len(ats) :]
    if not opening:
        sums, refs = refs[0], refs[1:]
    if closing:
        scales, refs = refs[:2], refs[2:]
    for who in range(shares):
        tall = slice(who * SHARE, (who + 1) * SHARE)
        past = slice((who + closing * 2 - 2) * SHARE, (who + closing * 2 - 1) * SHARE) if closing else tall
        total = None if opening else sums[past, :]
        for at, some in zip(ats, rows):
            term = jnp.dot(tokens[who][:, at : at + some.shape[0]], some[...], preferred_element_type=F32)
            total = term if total is None else total + term
        if closing:
            refs[0][tall, :] = (total * scales[who][:, 0:1]).astype(BF16)
        else:
            refs[0][tall, :] = total


def product(tokens, rows, state, ats, scales=(), closing=0):
    opening = state is None
    out = pltpu.VMEM((512, HALF), BF16) if closing else pltpu.VMEM((1024, HALF), F32)
    body = functools.partial(product_body, opening, closing, ats)
    operands = (*tokens, *rows, *(() if opening else (state,)), *scales)
    return call(body, operands, out)


def combine(own, other, out):
    c = lax.axis_index("c")

    @pl.when(c == 0)
    def _():
        out[:, 0:HALF] = own[...]
        out[:, HALF:] = other[...]

    @pl.when(c == 1)
    def _():
        out[:, 0:HALF] = other[...]
        out[:, HALF:] = own[...]


def per_device(tokens, gain, weight, down, up):
    zh, y, x, zl, c = (lax.axis_index(a) for a in AXES)
    down, up = down[0], up[0]

    down_other = send(down, to_core)
    parts = call(
        prepare,
        (down, down_other, up, weight),
        [pltpu.VMEM((96, HALF), BF16)] * 4 + [pltpu.VMEM((32, HALF), BF16)] * 2,
        [pltpu.VMEM((512, 128), BF16), pltpu.SemaphoreType.DMA((2,))],
        free=(0, 2),
        far=(3,),
    )
    weight_own, weight_other = parts[4], send(parts[5], to_core)
    parts = [parts[0]] + [send(parts[k], along_zh(k)) for k in (2, 1, 3)]
    gain = after(gain, parts[0])
    row = y * 128 + zh * 32
    tokens_other = send(after(tokens, down_other), to_core)
    start = (x * 2 + zl) * 1024 + row
    gains = [lax.dynamic_slice(gain, (start + who * HALF,), (32,)) for who in (c, 1 - c)]
    gains = jnp.broadcast_to(jnp.concatenate(gains).astype(F32)[:, None], (64, HALF))

    staged = [stage(after(tokens, parts[0]), 0), stage(tokens, 1), stage(tokens_other, 0), stage(tokens_other, 1)]
    every, scales = zip(*staged)

    parts = [after(parts[0], every[0], gains, weight_other), *parts[1:]]
    sums = call(partial_sums, parts, [pltpu.VMEM((64, HALF), F32)] * 4, [pltpu.VMEM((256, HALF), F32)])
    sums = [sums[0]] + [send(sums[k], along_y(k)) for k in (1, 3, 2)]
    sums = [after(sums[0], every[1]), *sums[1:]]
    merged = call(merge, (weight_own, weight_other, gains, *sums), pltpu.VMEM((64, HALF), BF16))
    merged = [merged] + [send(merged, along_zh(k)) for k in (2, 1, 3)]
    merged = [after(merged[0], every[2]), merged[2], merged[1], merged[3]]
    chunk = call(assemble, merged, pltpu.VMEM((256, HALF), BF16))

    whole, slab = pltpu.VMEM((1024, HALF), BF16), pltpu.VMEM((512, HALF), BF16)
    near = [send(chunk, first(k)) for k in (1, 2, 3)]
    here0, up0, low0 = call(join, [after(chunk, every[3]), *near], [whole, slab, slab])

    here1 = send(here0, beside)
    left_low0, right_low0 = send(low0, last(-1)), send(low0, last(1))
    left_up0, right_up0 = send(up0, last(-1)), send(up0, last(1))
    state = product(every, (here0,), None, (0,))
    left_low0 = after(left_low0, state)
    left_low1 = send(left_low0, beside)
    right_low0 = after(right_low0, left_low0)
    far_low0 = send(after(left_low0, right_low0), last(-1))
    here1 = after(here1, right_low0)
    up1 = call(upper, (here1,), slab)
    right_up1 = send(up1, last(1))
    left_up0 = after(left_up0, up1)
    left_up1 = send(after(up1, left_up0), last(-1))
    right_up0 = after(right_up0, left_up0)
    far_up0 = send(right_up0, last(1))
    left_low1 = after(left_low1, right_up0)
    far_low1 = send(left_low1, last(-1))
    far_low0 = after(far_low0, left_low1)
    right_low1 = send(after(right_low0, far_low0), beside)
    right_up1 = after(right_up1, far_low0)
    far_up1 = send(right_up1, last(1))
    state = product(every, (here1,), after(state, right_up1), (1024,))
    state = product(every, (left_up0, left_low0), state, (6144, 6656))
    state = product(every, (right_up0, right_low0), state, (2048, 2560))
    left_up1 = after(left_up1, state)
    state = product(every, (left_up1, left_low1), state, (7168, 7680))
    far_up0 = after(far_up0, state)
    state = product(every, (far_up0, far_low0), state, (4096, 4608))
    right_low1 = after(right_low1, state)
    state = product(every, (right_up1, right_low1), state, (3072, 3584))
    far_low1 = after(far_low1, state)
    ending, ats = (far_up1, far_low1), (5120, 5632)
    theirs = product(every[2:], ending, state, ats, scales[2:], 2)
    back = send(theirs, to_core)
    mine = product(every[:2], ending, state, ats, scales[:2], 1)
    return call(combine, (mine, back), shape(512, 2 * HALF))


def shape(rows, columns, dtype=BF16):
    return jax.ShapeDtypeStruct((rows, columns), dtype)


def solution(mesh):
    fine = Mesh(mesh.devices.reshape(SIZES), AXES)
    rows = ("x", "zl", "c")
    placed = (
        P(AXES, None),
        P(),
        P(rows, None),
        P(("zh", "y"), rows, None),
        P(("zh", "y"), None, None, None),
    )
    return jax.shard_map(per_device, mesh=fine, in_specs=placed, out_specs=P(AXES, None), check_vma=False)
```

```python
import functools

import jax
import jax.numpy as jnp
from jax import lax
from jax.experimental import pallas as pl
from jax.experimental.pallas import tpu as pltpu
from jax.sharding import Mesh, PartitionSpec as P

AXES = ("zh", "y", "x", "zl", "c")
SIZES = (4, 4, 4, 2, 2)
RANK = 64
HALF = 512
EPS = 1e-05
FEATURES = 8192
F32 = jnp.float32
BF16 = jnp.bfloat16


def pairs(move):
    out = []
    for src in range(256):
        core, rest = src % 2, src // 2
        zl, rest = rest % 2, rest // 2
        x, rest = rest % 4, rest // 4
        y, zh = rest % 4, rest // 4
        zh2, y2, x2, zl2, core2 = move(zh, y, x, zl, core)
        out.append((src, (((zh2 % 4 * 4 + y2 % 4) * 4 + x2 % 4) * 2 + zl2) * 2 + core2))
    return out


def send(array, move):
    return lax.ppermute(array, AXES, pairs(move))


def to_core(zh, y, x, zl, c):
    return zh, y, x, zl, 1 - c


def beside(zh, y, x, zl, c):
    if c == 0:
        return zh, y, x, 1 - zl, c
    return (zh - 1, y, x, 1, c) if zl == 0 else (zh + 1, y, x, 0, c)


def along_zh(k):
    return lambda zh, y, x, zl, c: (zh + k, y, x, zl, c)


def along_y(k):
    return lambda zh, y, x, zl, c: (zh, y + k, x, zl, c)


def first(k):
    return lambda zh, y, x, zl, c: (zh, y + k, x, zl, c) if c == 0 else (zh, y, x + k, zl, c)


def last(k):
    return lambda zh, y, x, zl, c: (zh, y, x + k, zl, c) if c == 0 else (zh, y + k, x, zl, c)


def after(array, *others):
    return lax.optimization_barrier((array, *others))[0]


VMEM = pl.BlockSpec(memory_space=pltpu.VMEM)


def call(body, operands, outs, scratch=(), cost=1024, flops=1024, free=()):
    operands = [
        pltpu.with_memory_space_constraint(a, pltpu.HBM if i in free else pltpu.VMEM) for i, a in enumerate(operands)
    ]
    return pl.pallas_call(
        body,
        out_shape=outs,
        in_specs=[VMEM] * len(operands),
        out_specs=jax.tree.map(lambda _: VMEM, outs),
        scratch_shapes=list(scratch),
        compiler_params=pltpu.CompilerParams(vmem_limit_bytes=16 << 20),
        cost_estimate=pl.CostEstimate(flops=flops, bytes_accessed=cost, transcendentals=0),
    )(*operands)


def prepare(own, other, up, *rest):
    outs, packed = rest[:4], rest[4]
    zh, c = lax.axis_index("zh"), lax.axis_index("c")
    mine, theirs = own[...].astype(F32), other[...].astype(F32)
    turned = jnp.where(c == 0, theirs, mine)
    turned = pltpu.roll(turned, RANK, 1)
    lane = lax.broadcasted_iota(jnp.int32, mine.shape, 1)
    low = jnp.where(c == 0, mine, turned)
    high = jnp.where(c == 0, turned, theirs)
    packed[...] = jnp.where(lane < RANK, low, high).astype(BF16)
    factor = up[pl.ds(c, 1)][0]
    for k in range(4):
        start = lax.rem(zh + k, 4) * 32
        outs[k][0:64, :] = factor
        for y in range(4):
            rows = pl.ds(pl.multiple_of(start + y * 128, 32), 32)
            outs[k][64:96, y * 128 : (y + 1) * 128] = packed[rows, :]


def partial_sums(*rest):
    parts, outs, total = rest[:4], rest[4:8], rest[8]
    y = lax.axis_index("y")
    lane = lax.broadcasted_iota(jnp.int32, (128, 128), 1)
    zero = jnp.zeros((128, 128), BF16)
    lefts, rights = [], []
    for part in parts:
        down = jnp.concatenate([part[64:96, j * 128 : (j + 1) * 128] for j in range(4)], axis=0)
        low = jnp.where(lane < RANK, down, zero)
        high = jnp.where(lane < RANK, zero, down)
        lefts.append(jnp.concatenate([low, high], axis=0))
        rights += [part[0:64, :]] * 2
    left = jnp.concatenate(lefts, axis=1)
    right = jnp.concatenate(rights, axis=0)
    total[...] = jnp.dot(left, right, preferred_element_type=F32)
    for k in range(4):
        start = pl.multiple_of(lax.rem(y + k, 4) * 32, 32)
        outs[k][0:32, :] = total[pl.ds(start, 32), :]
        outs[k][32:64, :] = total[pl.ds(start + 128, 32), :]


def merge(own, other, gain, a, b, c, d, out):
    update = 0.25 * ((a[...] + b[...]) + (c[...] + d[...]))
    out[0:32, :] = ((own[...].astype(F32) + update[0:32]) * gain[0:32]).astype(BF16)
    out[32:64, :] = ((other[...].astype(F32) + update[32:64]) * gain[32:64]).astype(BF16)


def assemble(*refs):
    parts, out = refs[:4], refs[4]
    zh = lax.axis_index("zh")
    for k in range(4):
        start = pl.multiple_of(lax.rem(zh + 4 - k, 4) * 32, 32)
        out[pl.ds(start, 32), :] = parts[k][0:32, :]
        out[pl.ds(start + 128, 32), :] = parts[k][32:64, :]


def join(*refs):
    parts, whole, mine, theirs = refs[:4], refs[4], refs[5], refs[6]
    for k in range(4):
        at, below = slice(k * 128, (k + 1) * 128), slice(512 + k * 128, 512 + (k + 1) * 128)
        whole[at, :] = mine[at, :] = parts[k][0:128, :]
        whole[below, :] = theirs[at, :] = parts[k][128:256, :]


def upper(rows, out):
    out[...] = rows[0:512, :]


def strip(place):
    y, x, zl, c = (lax.axis_index(a) for a in AXES[1:])
    block, part, core, step = place // 16, place // 8 % 2, place // 4 % 2, place % 4
    far = jnp.where(c == 0, x, y)
    near = jnp.where(c == 0, y, x)
    far = lax.rem(far + 4 - block, 4)
    near = lax.rem(near + 4 - step, 4)
    row_x = jnp.where(c == 0, far, near)
    row_y = jnp.where(c == 0, near, far)
    zl = zl if part == 0 else 1 - zl
    core = c if core == 0 else 1 - c
    return row_x * 16 + zl * 8 + core * 4 + row_y


TALL = 64
SHARE = 256


def stage_body(tokens, out, scale):
    at = pl.ds(pl.multiple_of(pl.program_id(0) * TALL, TALL), TALL)
    square = jnp.zeros((TALL, 128), F32)
    for place in range(64):
        column = pl.ds(pl.multiple_of(strip(place) * 128, 128), 128)
        piece = tokens[:, column]
        out[at, place * 128 : (place + 1) * 128] = piece
        value = piece.astype(F32)
        square = square + value * value
    mean = jnp.sum(square, axis=1, keepdims=True) / FEATURES
    scale[at, :] = jnp.broadcast_to(lax.rsqrt(mean + EPS), (TALL, 128))


def stage(tokens, share):
    steps = SHARE // TALL
    return pl.pallas_call(
        stage_body,
        grid=(steps,),
        out_shape=[pltpu.VMEM((SHARE, FEATURES), BF16), pltpu.VMEM((SHARE, 128), F32)],
        in_specs=[pl.BlockSpec((TALL, FEATURES), lambda i: (i + share * steps, 0))],
        out_specs=[VMEM] * 2,
        compiler_params=pltpu.CompilerParams(vmem_limit_bytes=16 << 20),
        cost_estimate=pl.CostEstimate(flops=1 << 24, bytes_accessed=8 << 20, transcendentals=0),
    )(pltpu.with_memory_space_constraint(tokens, pltpu.HBM))


def product_body(opening, closing, ats, *refs):
    shares = 2 if closing else 4
    tokens, rows, refs = refs[:shares], refs[shares : shares + len(ats)], refs[shares + len(ats) :]
    if not opening:
        sums, refs = refs[0], refs[1:]
    if closing:
        scales, refs = refs[:2], refs[2:]
    for who in range(shares):
        tall = slice(who * SHARE, (who + 1) * SHARE)
        past = slice((who + closing * 2 - 2) * SHARE, (who + closing * 2 - 1) * SHARE) if closing else tall
        total = None if opening else sums[past, :]
        for at, some in zip(ats, rows):
            term = jnp.dot(tokens[who][:, at : at + some.shape[0]], some[...], preferred_element_type=F32)
            total = term if total is None else total + term
        if closing:
            refs[0][tall, :] = (total * scales[who][:, 0:1]).astype(BF16)
        else:
            refs[0][tall, :] = total


def product(tokens, rows, state, ats, scales=(), closing=0):
    opening = state is None
    out = pltpu.VMEM((512, HALF), BF16) if closing else pltpu.VMEM((1024, HALF), F32)
    body = functools.partial(product_body, opening, closing, ats)
    operands = (*tokens, *rows, *(() if opening else (state,)), *scales)
    return call(body, operands, out)


def combine(own, other, out):
    c = lax.axis_index("c")

    @pl.when(c == 0)
    def _():
        out[:, 0:HALF] = own[...]
        out[:, HALF:] = other[...]

    @pl.when(c == 1)
    def _():
        out[:, 0:HALF] = other[...]
        out[:, HALF:] = own[...]


def per_device(tokens, gain, weight, down, up):
    zh, y, x, zl, c = (lax.axis_index(a) for a in AXES)
    down, up = down[0], up[0]

    down_other = send(down, to_core)
    parts = call(
        prepare,
        (down, down_other, up),
        [pltpu.VMEM((96, HALF), BF16)] * 4,
        [pltpu.VMEM((512, 128), BF16)],
        free=(0, 2),
    )
    parts = [parts[0]] + [send(parts[k], along_zh(k)) for k in (2, 1, 3)]
    gain = after(gain, parts[0])
    row = y * 128 + zh * 32
    weight_own = lax.dynamic_slice(weight, (row, c * HALF), (32, HALF))
    weight_other = lax.dynamic_slice(weight, (row, (1 - c) * HALF), (32, HALF))
    weight_other = send(after(weight_other, parts[1]), to_core)
    tokens_other = send(after(tokens, down_other), to_core)
    start = (x * 2 + zl) * 1024 + row
    gains = [lax.dynamic_slice(gain, (start + who * HALF,), (32,)) for who in (c, 1 - c)]
    gains = jnp.broadcast_to(jnp.concatenate(gains).astype(F32)[:, None], (64, HALF))

    staged = [stage(after(tokens, parts[0]), 0), stage(tokens, 1), stage(tokens_other, 0), stage(tokens_other, 1)]
    every, scales = zip(*staged)

    parts = [after(parts[0], every[0], gains), *parts[1:]]
    sums = call(partial_sums, parts, [pltpu.VMEM((64, HALF), F32)] * 4, [pltpu.VMEM((256, HALF), F32)])
    sums = [sums[0]] + [send(sums[k], along_y(k)) for k in (1, 3, 2)]
    sums = [after(sums[0], every[1]), *sums[1:]]
    merged = call(merge, (weight_own, weight_other, gains, *sums), pltpu.VMEM((64, HALF), BF16))
    merged = [merged] + [send(merged, along_zh(k)) for k in (2, 1, 3)]
    merged = [after(merged[0], every[2]), merged[2], merged[1], merged[3]]
    chunk = call(assemble, merged, pltpu.VMEM((256, HALF), BF16))

    whole, slab = pltpu.VMEM((1024, HALF), BF16), pltpu.VMEM((512, HALF), BF16)
    near = [send(chunk, first(k)) for k in (1, 2, 3)]
    here0, up0, low0 = call(join, [after(chunk, every[3]), *near], [whole, slab, slab])

    here1 = send(here0, beside)
    left_low0, right_low0 = send(low0, last(-1)), send(low0, last(1))
    left_up0, right_up0 = send(up0, last(-1)), send(up0, last(1))
    state = product(every, (here0,), None, (0,))
    left_low0 = after(left_low0, state)
    left_low1 = send(left_low0, beside)
    right_low0 = after(right_low0, left_low0)
    far_low0 = send(after(left_low0, right_low0), last(-1))
    here1 = after(here1, right_low0)
    up1 = call(upper, (here1,), slab)
    right_up1 = send(up1, last(1))
    left_up0 = after(left_up0, up1)
    left_up1 = send(after(up1, left_up0), last(-1))
    right_up0 = after(right_up0, left_up0)
    far_up0 = send(right_up0, last(1))
    left_low1 = after(left_low1, right_up0)
    far_low1 = send(left_low1, last(-1))
    far_low0 = after(far_low0, left_low1)
    right_low1 = send(after(right_low0, far_low0), beside)
    right_up1 = after(right_up1, far_low0)
    far_up1 = send(right_up1, last(1))
    state = product(every, (here1,), after(state, right_up1), (1024,))
    state = product(every, (left_up0, left_low0), state, (6144, 6656))
    state = product(every, (right_up0, right_low0), state, (2048, 2560))
    left_up1 = after(left_up1, state)
    state = product(every, (left_up1, left_low1), state, (7168, 7680))
    far_up0 = after(far_up0, state)
    state = product(every, (far_up0, far_low0), state, (4096, 4608))
    right_low1 = after(right_low1, state)
    state = product(every, (right_up1, right_low1), state, (3072, 3584))
    far_low1 = after(far_low1, state)
    ending, ats = (far_up1, far_low1), (5120, 5632)
    theirs = product(every[2:], ending, state, ats, scales[2:], 2)
    back = send(theirs, to_core)
    mine = product(every[:2], ending, state, ats, scales[:2], 1)
    return call(combine, (mine, back), shape(512, 2 * HALF))


def shape(rows, columns, dtype=BF16):
    return jax.ShapeDtypeStruct((rows, columns), dtype)


def solution(mesh):
    fine = Mesh(mesh.devices.reshape(SIZES), AXES)
    rows = ("x", "zl", "c")
    placed = (
        P(AXES, None),
        P(),
        P(rows, None),
        P(("zh", "y"), rows, None),
        P(("zh", "y"), None, None, None),
    )
    return jax.shard_map(per_device, mesh=fine, in_specs=placed, out_specs=P(AXES, None), check_vma=False)
```

```python
import functools

import jax
import jax.numpy as jnp
from jax import lax
from jax.experimental import pallas as pl
from jax.experimental.pallas import tpu as pltpu
from jax.sharding import Mesh, PartitionSpec as P

AXES = ("zh", "y", "x", "zl", "c")
SIZES = (4, 4, 4, 2, 2)
RANK = 64
HALF = 512
EPS = 1e-05
FEATURES = 8192
F32 = jnp.float32
BF16 = jnp.bfloat16


def pairs(move):
    out = []
    for src in range(256):
        core, rest = src % 2, src // 2
        zl, rest = rest % 2, rest // 2
        x, rest = rest % 4, rest // 4
        y, zh = rest % 4, rest // 4
        zh2, y2, x2, zl2, core2 = move(zh, y, x, zl, core)
        out.append((src, (((zh2 % 4 * 4 + y2 % 4) * 4 + x2 % 4) * 2 + zl2) * 2 + core2))
    return out


def send(array, move):
    return lax.ppermute(array, AXES, pairs(move))


def to_core(zh, y, x, zl, c):
    return zh, y, x, zl, 1 - c


def beside(zh, y, x, zl, c):
    if c == 0:
        return zh, y, x, 1 - zl, c
    return (zh - 1, y, x, 1, c) if zl == 0 else (zh + 1, y, x, 0, c)


def along_zh(k):
    return lambda zh, y, x, zl, c: (zh + k, y, x, zl, c)


def along_y(k):
    return lambda zh, y, x, zl, c: (zh, y + k, x, zl, c)


def first(k):
    return lambda zh, y, x, zl, c: (zh, y + k, x, zl, c) if c == 0 else (zh, y, x + k, zl, c)


def last(k):
    return lambda zh, y, x, zl, c: (zh, y, x + k, zl, c) if c == 0 else (zh, y + k, x, zl, c)


def after(array, *others):
    return lax.optimization_barrier((array, *others))[0]


VMEM = pl.BlockSpec(memory_space=pltpu.VMEM)


def call(body, operands, outs, scratch=(), cost=1024, flops=1024, free=()):
    operands = [
        pltpu.with_memory_space_constraint(a, pltpu.HBM if i in free else pltpu.VMEM) for i, a in enumerate(operands)
    ]
    return pl.pallas_call(
        body,
        out_shape=outs,
        in_specs=[VMEM] * len(operands),
        out_specs=jax.tree.map(lambda _: VMEM, outs),
        scratch_shapes=list(scratch),
        compiler_params=pltpu.CompilerParams(vmem_limit_bytes=16 << 20),
        cost_estimate=pl.CostEstimate(flops=flops, bytes_accessed=cost, transcendentals=0),
    )(*operands)


def prepare(own, other, up, *rest):
    outs, packed = rest[:4], rest[4]
    zh, c = lax.axis_index("zh"), lax.axis_index("c")
    mine, theirs = own[...].astype(F32), other[...].astype(F32)
    turned = jnp.where(c == 0, theirs, mine)
    turned = pltpu.roll(turned, RANK, 1)
    lane = lax.broadcasted_iota(jnp.int32, mine.shape, 1)
    low = jnp.where(c == 0, mine, turned)
    high = jnp.where(c == 0, turned, theirs)
    packed[...] = jnp.where(lane < RANK, low, high).astype(BF16)
    factor = up[pl.ds(c, 1)][0]
    for k in range(4):
        start = lax.rem(zh + k, 4) * 32
        outs[k][0:64, :] = factor
        for y in range(4):
            rows = pl.ds(pl.multiple_of(start + y * 128, 32), 32)
            outs[k][64:96, y * 128 : (y + 1) * 128] = packed[rows, :]


def partial_sums(*rest):
    parts, outs, total = rest[:4], rest[4:8], rest[8]
    y = lax.axis_index("y")
    lane = lax.broadcasted_iota(jnp.int32, (128, 128), 1)
    zero = jnp.zeros((128, 128), BF16)
    lefts, rights = [], []
    for part in parts:
        down = jnp.concatenate([part[64:96, j * 128 : (j + 1) * 128] for j in range(4)], axis=0)
        low = jnp.where(lane < RANK, down, zero)
        high = jnp.where(lane < RANK, zero, down)
        lefts.append(jnp.concatenate([low, high], axis=0))
        rights += [part[0:64, :]] * 2
    left = jnp.concatenate(lefts, axis=1)
    right = jnp.concatenate(rights, axis=0)
    total[...] = jnp.dot(left, right, preferred_element_type=F32)
    for k in range(4):
        start = pl.multiple_of(lax.rem(y + k, 4) * 32, 32)
        outs[k][0:32, :] = total[pl.ds(start, 32), :]
        outs[k][32:64, :] = total[pl.ds(start + 128, 32), :]


def merge(own, other, gain, a, b, c, d, out):
    update = 0.25 * ((a[...] + b[...]) + (c[...] + d[...]))
    out[0:32, :] = ((own[...].astype(F32) + update[0:32]) * gain[0:32]).astype(BF16)
    out[32:64, :] = ((other[...].astype(F32) + update[32:64]) * gain[32:64]).astype(BF16)


def assemble(*refs):
    parts, out = refs[:4], refs[4]
    zh = lax.axis_index("zh")
    for k in range(4):
        start = pl.multiple_of(lax.rem(zh + 4 - k, 4) * 32, 32)
        out[pl.ds(start, 32), :] = parts[k][0:32, :]
        out[pl.ds(start + 128, 32), :] = parts[k][32:64, :]


def join(*refs):
    parts, whole, mine, theirs = refs[:4], refs[4], refs[5], refs[6]
    for k in range(4):
        at, below = slice(k * 128, (k + 1) * 128), slice(512 + k * 128, 512 + (k + 1) * 128)
        whole[at, :] = mine[at, :] = parts[k][0:128, :]
        whole[below, :] = theirs[at, :] = parts[k][128:256, :]


def upper(rows, out):
    out[...] = rows[0:512, :]


def strip(place):
    y, x, zl, c = (lax.axis_index(a) for a in AXES[1:])
    block, part, core, step = place // 16, place // 8 % 2, place // 4 % 2, place % 4
    far = jnp.where(c == 0, x, y)
    near = jnp.where(c == 0, y, x)
    far = lax.rem(far + 4 - block, 4)
    near = lax.rem(near + 4 - step, 4)
    row_x = jnp.where(c == 0, far, near)
    row_y = jnp.where(c == 0, near, far)
    zl = zl if part == 0 else 1 - zl
    core = c if core == 0 else 1 - c
    return row_x * 16 + zl * 8 + core * 4 + row_y


TALL = 64
SHARE = 256


def stage_body(tokens, out, scale):
    at = pl.ds(pl.multiple_of(pl.program_id(0) * TALL, TALL), TALL)
    square = jnp.zeros((TALL, 128), F32)
    for place in range(64):
        column = pl.ds(pl.multiple_of(strip(place) * 128, 128), 128)
        piece = tokens[:, column]
        out[at, place * 128 : (place + 1) * 128] = piece
        value = piece.astype(F32)
        square = square + value * value
    mean = jnp.sum(square, axis=1, keepdims=True) / FEATURES
    scale[at, :] = jnp.broadcast_to(lax.rsqrt(mean + EPS), (TALL, 128))


def stage(tokens, share):
    steps = SHARE // TALL
    return pl.pallas_call(
        stage_body,
        grid=(steps,),
        out_shape=[pltpu.VMEM((SHARE, FEATURES), BF16), pltpu.VMEM((SHARE, 128), F32)],
        in_specs=[pl.BlockSpec((TALL, FEATURES), lambda i: (i + share * steps, 0))],
        out_specs=[VMEM] * 2,
        compiler_params=pltpu.CompilerParams(vmem_limit_bytes=16 << 20),
        cost_estimate=pl.CostEstimate(flops=1 << 24, bytes_accessed=8 << 20, transcendentals=0),
    )(pltpu.with_memory_space_constraint(tokens, pltpu.HBM))


def product_body(opening, closing, ats, *refs):
    shares = 2 if closing else 4
    tokens, rows, refs = refs[:shares], refs[shares : shares + len(ats)], refs[shares + len(ats) :]
    if not opening:
        sums, refs = refs[0], refs[1:]
    if closing:
        scales, refs = refs[:2], refs[2:]
    for who in range(shares):
        tall = slice(who * SHARE, (who + 1) * SHARE)
        past = slice((who + closing * 2 - 2) * SHARE, (who + closing * 2 - 1) * SHARE) if closing else tall
        total = None if opening else sums[past, :]
        for at, some in zip(ats, rows):
            term = jnp.dot(tokens[who][:, at : at + some.shape[0]], some[...], preferred_element_type=F32)
            total = term if total is None else total + term
        if closing:
            refs[0][tall, :] = (total * scales[who][:, 0:1]).astype(BF16)
        else:
            refs[0][tall, :] = total


def product(tokens, rows, state, ats, scales=(), closing=0):
    opening = state is None
    out = pltpu.VMEM((512, HALF), BF16) if closing else pltpu.VMEM((1024, HALF), F32)
    body = functools.partial(product_body, opening, closing, ats)
    operands = (*tokens, *rows, *(() if opening else (state,)), *scales)
    return call(body, operands, out)


def combine(own, other, out):
    c = lax.axis_index("c")

    @pl.when(c == 0)
    def _():
        out[:, 0:HALF] = own[...]
        out[:, HALF:] = other[...]

    @pl.when(c == 1)
    def _():
        out[:, 0:HALF] = other[...]
        out[:, HALF:] = own[...]


def per_device(tokens, gain, weight, down, up):
    zh, y, x, zl, c = (lax.axis_index(a) for a in AXES)
    down, up = down[0], up[0]

    down_other = send(down, to_core)
    parts = call(
        prepare,
        (down, down_other, up),
        [pltpu.VMEM((96, HALF), BF16)] * 4,
        [pltpu.VMEM((512, 128), BF16)],
        free=(0, 2),
    )
    parts = [parts[0]] + [send(parts[k], along_zh(k)) for k in (2, 1, 3)]
    gain = after(gain, parts[0])
    row = y * 128 + zh * 32
    weight_own = lax.dynamic_slice(weight, (row, c * HALF), (32, HALF))
    weight_other = lax.dynamic_slice(weight, (row, (1 - c) * HALF), (32, HALF))
    weight_other = send(after(weight_other, parts[1]), to_core)
    tokens_other = send(after(tokens, down_other), to_core)
    start = (x * 2 + zl) * 1024 + row
    gains = [lax.dynamic_slice(gain, (start + who * HALF,), (32,)) for who in (c, 1 - c)]
    gains = jnp.broadcast_to(jnp.concatenate(gains).astype(F32)[:, None], (64, HALF))

    staged = [stage(after(tokens, parts[0]), 0), stage(tokens, 1), stage(tokens_other, 0), stage(tokens_other, 1)]
    every, scales = zip(*staged)

    parts = [after(parts[0], every[0], gains), *parts[1:]]
    sums = call(partial_sums, parts, [pltpu.VMEM((64, HALF), F32)] * 4, [pltpu.VMEM((256, HALF), F32)])
    sums = [sums[0]] + [send(sums[k], along_y(k)) for k in (1, 3, 2)]
    sums = [after(sums[0], every[1]), *sums[1:]]
    merged = call(merge, (weight_own, weight_other, gains, *sums), pltpu.VMEM((64, HALF), BF16))
    merged = [merged] + [send(merged, along_zh(k)) for k in (2, 1, 3)]
    merged = [after(merged[0], every[2]), merged[2], merged[1], merged[3]]
    chunk = call(assemble, merged, pltpu.VMEM((256, HALF), BF16))

    whole, slab = pltpu.VMEM((1024, HALF), BF16), pltpu.VMEM((512, HALF), BF16)
    near = [send(chunk, first(k)) for k in (1, 2, 3)]
    here0, up0, low0 = call(join, [after(chunk, every[3]), *near], [whole, slab, slab])

    here1 = send(here0, beside)
    left_low0, right_low0 = send(low0, last(-1)), send(low0, last(1))
    left_up0, right_up0 = send(up0, last(-1)), send(up0, last(1))
    state = product(every, (here0,), None, (0,))
    left_low0 = after(left_low0, state)
    left_low1 = send(left_low0, beside)
    right_low0 = after(right_low0, left_low0)
    far_low0 = send(after(left_low0, right_low0), last(-1))
    here1 = after(here1, right_low0)
    up1 = call(upper, (here1,), slab)
    right_up1 = send(up1, last(1))
    left_up0 = after(left_up0, up1)
    left_up1 = send(after(up1, left_up0), last(-1))
    right_up0 = after(right_up0, left_up0)
    far_up0 = send(right_up0, last(1))
    left_low1 = after(left_low1, right_up0)
    far_low1 = send(left_low1, last(-1))
    far_low0 = after(far_low0, left_low1)
    right_low1 = send(after(right_low0, far_low0), beside)
    right_up1 = after(right_up1, far_low0)
    far_up1 = send(right_up1, last(1))
    state = product(every, (here1,), after(state, right_up1), (1024,))
    state = product(every, (left_up0, left_low0), state, (6144, 6656))
    state = product(every, (right_up0, right_low0), state, (2048, 2560))
    left_up1 = after(left_up1, state)
    state = product(every, (left_up1, left_low1), state, (7168, 7680))
    far_up0 = after(far_up0, state)
    state = product(every, (far_up0, far_low0), state, (4096, 4608))
    right_low1 = after(right_low1, state)
    state = product(every, (right_up1, right_low1), state, (3072, 3584))
    far_low1 = after(far_low1, state)
    state = product(every, (far_low1,), state, (5632,))
    far_up1 = after(far_up1, state)
    ending, ats = (far_up1,), (5120,)
    theirs = product(every[2:], ending, state, ats, scales[2:], 2)
    back = send(theirs, to_core)
    mine = product(every[:2], ending, state, ats, scales[:2], 1)
    return call(combine, (mine, back), shape(512, 2 * HALF))


def shape(rows, columns, dtype=BF16):
    return jax.ShapeDtypeStruct((rows, columns), dtype)


def solution(mesh):
    fine = Mesh(mesh.devices.reshape(SIZES), AXES)
    rows = ("x", "zl", "c")
    placed = (
        P(AXES, None),
        P(),
        P(rows, None),
        P(("zh", "y"), rows, None),
        P(("zh", "y"), None, None, None),
    )
    return jax.shard_map(per_device, mesh=fine, in_specs=placed, out_specs=P(AXES, None), check_vma=False)
```
